32 devices in a mesh: dp: 8 (over z, x), tensor: 4 (over y, core).
Axes of the slice: x: 2, y: 2, z: 4, core: 2. Of those that a mesh axis runs over, the one named last changes fastest.
Arguments:
- tokens: bfloat16 [4096, 1024], P(('dp', 'tensor')), may hold values from -6 to 6
- cotangent: bfloat16 [4096, 1024], P(('dp', 'tensor')), may hold values from -6 to 6
- segments: int32 [4096], P('dp'), may hold values from 0 to 2, as said below
- routes: int32 [4096, 8], P('dp'), may hold values from 0 to 15, all different within a row; in each aligned block of 512 rows (0 to 511, 512 to 1023, ...) at most 288 rows name the same one
- attn_gain: bfloat16 [1024], P('dp'), may hold values from 0.5 to 1.5
- query_matrix: bfloat16 [1024, 1024], P('dp', 'tensor'), may hold values from -0.1875 to 0.1875
- key_matrix: bfloat16 [1024, 512], P('dp', 'tensor'), may hold values from -0.1875 to 0.1875
- value_matrix: bfloat16 [1024, 512], P('dp', 'tensor'), may hold values from -0.1875 to 0.1875
- w_out: bfloat16 [1024, 1024], P('tensor', 'dp'), may hold values from -1.5 to 1.5
- moe_gain: bfloat16 [1024], P('dp'), may hold values from 0.5 to 1.5
- w_router: bfloat16 [1024, 16], P('dp'), may hold values from -0.09375 to 0.09375
- w_gate: bfloat16 [16, 1024, 512], P(None, 'dp', 'tensor'), may hold values from -0.1875 to 0.1875
- w_up: bfloat16 [16, 1024, 512], P(None, 'dp', 'tensor'), may hold values from -0.1875 to 0.1875
- w_down: bfloat16 [16, 512, 1024], P(None, 'tensor', 'dp'), may hold values from -1 to 1
Outputs:
- output: bfloat16 [4096, 1024], P(('dp', 'tensor'))
- input_grad: float32 [4096, 1024], P(('dp', 'tensor'))
- grad_attn_gain: float32 [1024], P('dp')
- grad_w_query: float32 [1024, 1024], P('dp', 'tensor')
- grad_w_key: float32 [1024, 512], P('dp', 'tensor')
- grad_w_value: float32 [1024, 512], P('dp', 'tensor')
- grad_w_out: float32 [1024, 1024], P('tensor', 'dp')
- grad_moe_gain: float32 [1024], P('dp')
- grad_w_router: float32 [1024, 16], P('dp')
- grad_w_gate: float32 [16, 1024, 512], P(None, 'dp', 'tensor')
- grad_w_up: float32 [16, 1024, 512], P(None, 'dp', 'tensor')
- grad_w_down: float32 [16, 512, 1024], P(None, 'tensor', 'dp')
The draws below stay inside these ranges and needn't reach their ends.
Inputs may be any that keep to these rules, and one draw needn't show every extreme that they name: `segments`: within each block of 512 tokens (one index of dp) the numbers count the documents from 0 and never fall. `routes`: each row names 8 different experts; within the tokens of one index of dp (aligned blocks of 512 rows) no expert is named by more than 288 rows.
All inputs are finite; a program needn't handle non-finite values.
Results may differ from the reference program's by a relative error of at most 0.02.
Values may be sent and summed in bfloat16 or wider, within the bound.
A program may use at most 192 MiB of HBM per device.

```python
import math
import jax
import jax.numpy as jnp
import numpy as np
from jax import lax

MODEL_WIDTH = 1024
QUERY_HEADS = 16
KEY_VALUE_HEADS = 8
HEAD_SIZE = 64
FF = 512
EXPERTS = 16
K = 8
TOK_DEV = 512
CAP = 288
TOKENS = 4096
N_DP = 8


def draw_segments(key, part):
    key = jax.random.fold_in(key, 7)
    first_key, second_key = jax.random.split(key)
    begins = jax.random.randint(first_key, (N_DP, 1), 1, TOK_DEV // 8 + 1)
    endings = jax.random.randint(second_key, (N_DP, 1), 1, TOK_DEV // 8 + 1)
    places = jnp.arange(TOK_DEV, dtype=jnp.int32)[None, :]
    numbers = (places >= begins).astype(jnp.int32) + (places >= TOK_DEV - endings).astype(jnp.int32)
    return numbers.reshape(-1)


def steps_of(key, dims, cuts, low, top_value):
    loudness = 1.0
    for position, shards_of in cuts:
        heights = jax.random.uniform(jax.random.fold_in(jax.random.fold_in(key, 6), position), (shards_of,), jnp.float32, low / len(cuts), top_value / len(cuts))
        loudness = loudness * jnp.repeat(jnp.exp(heights), dims[position] // shards_of).reshape((-1,) + (1,) * (len(dims) - 1 - position))
    return loudness


def shared_out(own_key, own, number, rows, amount, top, most, slope):
    order = jax.random.permutation(own_key, amount)
    crowded, usual = load_shares(amount, rows * top, most, slope, True), load_shares(amount, rows * top, most, slope, False)
    places = jnp.arange(amount)

    def named(tallies, rotation):
        used = int((tallies > 0).sum())
        fixed = max(1, used // 4)
        moved = fixed + (places - fixed + rotation * (used - fixed)) % max(1, amount - fixed)
        return jnp.zeros((amount,), jnp.int32).at[order[jnp.where(places < fixed, places, moved)]].set(jnp.asarray(tallies, jnp.int32))

    tallies = jnp.where(number % 4 == 0, named(crowded, number // 4), named(usual, number - number // 4 - 1))
    mixed = jax.random.permutation(jax.random.fold_in(own, 3), amount)
    donor, sink = mixed[0:amount // 2 * 2:2], mixed[1:amount // 2 * 2:2]
    room = jnp.minimum(tallies[donor] - 1, most - tallies[sink]) // 2
    room = jnp.where((donor == order[0]) | (sink == order[0]) | (tallies[sink] == 0), 0, jnp.maximum(room, 0))
    moved = jax.random.randint(jax.random.fold_in(own, 4), (amount // 2,), 0, 1 << 20) % (room + 1)
    tallies = tallies.at[donor].add(-moved).at[sink].add(moved)
    members = jnp.searchsorted(jnp.cumsum(tallies), jnp.arange(rows * top), side="right").astype(jnp.int32)
    table = members.reshape(top, rows).T
    table = table[jax.random.permutation(jax.random.fold_in(own, 1), rows)]
    rotation = jax.random.randint(jax.random.fold_in(own, 2), (rows, 1), 0, top)
    return jnp.take_along_axis(table, (jnp.arange(top)[None, :] + rotation) % top, axis=1)


def load_shares(count, total, bound, lean, full):
    loads = [(1 << 20) // math.isqrt(grade ** lean) + 1 for grade in range(1, count + 1)]
    largest = bound if full else min(bound, max(-(-total // count), total * loads[0] // sum(loads)))
    least = 1 if total - largest >= count - 1 else 0
    counts, surplus = [largest] + [least] * (count - 1), total - largest - least * (count - 1)
    while surplus > 0:
        free = [i for i in range(1, count) if counts[i] < largest] or [i for i in range(1, count) if counts[i] < bound]
        pool, remaining = sum([loads[i] for i in free]), surplus
        for i in free:
            addition = min(bound - counts[i], max(1, remaining * loads[i] // pool), surplus)
            counts[i] = counts[i] + addition
            surplus = surplus - addition
    return np.array(counts)


def bell_draw(key, shape, scale, limit, cuts=(), held_as=jnp.bfloat16):
    values = jax.random.normal(key, shape, jnp.float32) * scale
    if len(cuts) > 0:
        values = steps_of(key, shape, cuts, -0.22, 0.18) * values
    return jnp.clip(values, min=-limit, max=limit).astype(held_as)


def setup_inputs(seed: int = 0) -> dict:
    arg_keys = jax.random.split(jax.random.key(seed), 15)
    tokens = bell_draw(arg_keys[0], (TOKENS, MODEL_WIDTH), 1.0, 6.0, ((0, 32),))
    cotangent = bell_draw(arg_keys[1], (TOKENS, MODEL_WIDTH), 1.0, 6.0, ((0, 32),))
    segments = draw_segments(jax.random.fold_in(arg_keys[14], 71), 0)
    routes_keys = jax.random.split(jax.random.fold_in(arg_keys[3], 1), TOKENS // TOK_DEV)
    routes_turns = jax.random.permutation(jax.random.fold_in(arg_keys[3], 3), TOKENS // TOK_DEV)
    routes = jax.vmap(lambda own, number: shared_out(jax.random.fold_in(arg_keys[3], 2), own, number, TOK_DEV, EXPERTS, K, CAP, 1))(routes_keys, routes_turns).reshape((TOKENS, K))
    attn_gain = jnp.clip(1.0 + 0.1 * jax.random.normal(arg_keys[4], (MODEL_WIDTH,), jnp.float32), 0.5, 1.5).astype(jnp.bfloat16)
    query_matrix = bell_draw(arg_keys[5], (MODEL_WIDTH, QUERY_HEADS * HEAD_SIZE), MODEL_WIDTH ** -0.5, 0.1875, ((0, 8), (1, 4)))
    key_matrix = bell_draw(arg_keys[6], (MODEL_WIDTH, KEY_VALUE_HEADS * HEAD_SIZE), MODEL_WIDTH ** -0.5, 0.1875, ((0, 8), (1, 4)))
    value_matrix = bell_draw(arg_keys[7], (MODEL_WIDTH, KEY_VALUE_HEADS * HEAD_SIZE), MODEL_WIDTH ** -0.5, 0.1875, ((0, 8), (1, 4)))
    w_out = bell_draw(arg_keys[8], (QUERY_HEADS * HEAD_SIZE, MODEL_WIDTH), 16 ** -0.5, 1.5, ((0, 4), (1, 8)))
    moe_gain = jnp.clip(1.0 + 0.1 * jax.random.normal(arg_keys[9], (MODEL_WIDTH,), jnp.float32), 0.5, 1.5).astype(jnp.bfloat16)
    w_router = bell_draw(arg_keys[10], (MODEL_WIDTH, EXPERTS), (4 * MODEL_WIDTH) ** -0.5, 0.09375, ((0, 8),))
    w_gate = bell_draw(arg_keys[11], (EXPERTS, MODEL_WIDTH, FF), MODEL_WIDTH ** -0.5, 0.1875, ((1, 8), (2, 4)))
    w_up = bell_draw(arg_keys[12], (EXPERTS, MODEL_WIDTH, FF), MODEL_WIDTH ** -0.5, 0.1875, ((1, 8), (2, 4)))
    w_down = bell_draw(arg_keys[13], (EXPERTS, FF, MODEL_WIDTH), (FF // 16) ** -0.5, 1.0, ((1, 4), (2, 8)))
    return {"tokens": tokens, "cotangent": cotangent, "segments": segments, "routes": routes, "attn_gain": attn_gain, "query_matrix": query_matrix, "key_matrix": key_matrix, "value_matrix": value_matrix, "w_out": w_out, "moe_gain": moe_gain, "w_router": w_router, "w_gate": w_gate, "w_up": w_up, "w_down": w_down}


@jax.custom_vjp
def low(v):
    return lax.optimization_barrier(v.astype(jnp.bfloat16)).astype(jnp.float32)

@jax.custom_vjp
def low_back(v):
    return v

def low_keep(v):
    return (low(v), None)

def low_pass(kept, grad):
    return (grad,)

def back_keep(v):
    return (v, None)

def back_low(kept, grad):
    return (low(grad),)
low.defvjp(low_keep, low_pass)
low_back.defvjp(back_keep, back_low)
norm_eps = 1e-06
masked_score = -1e+30
highest = lax.Precision.HIGHEST

def rounded_pair(values):
    return low(low_back(values))

def matrix_product(left, right):
    return jnp.dot(left, right, precision=highest)

def rms_scale(values, scales):
    return values * lax.rsqrt(lax.optimization_barrier(jnp.mean(values * values, axis=-1, keepdims=True)) + norm_eps) * scales

def route_gates(logits, route_ids):
    numbers = jnp.arange(logits.shape[1], dtype=jnp.int32)
    chosen = lax.optimization_barrier(jnp.sum(jnp.where(route_ids[:, :, None] == numbers[None, None, :], logits[:, None, :], 0.0), axis=2))
    shifted = jnp.exp(chosen - lax.optimization_barrier(jnp.max(chosen, axis=1, keepdims=True)))
    return shifted / lax.optimization_barrier(jnp.sum(shifted, axis=1, keepdims=True))

def dispatch_tables(route_ids, experts, capacity):
    token_total = route_ids.shape[0]
    top_count = route_ids.shape[1]
    flat_routes = route_ids.reshape(-1)
    matches = (flat_routes[:, None] == jnp.arange(experts, dtype=jnp.int32)[None, :]).astype(jnp.int32)
    running = jnp.cumsum(matches, axis=0)
    slot_index = lax.optimization_barrier(jnp.sum((running - 1) * matches, axis=1))
    targets = flat_routes * capacity + slot_index
    sources = jnp.arange(token_total * top_count, dtype=jnp.int32) // top_count
    owners = jnp.full((experts * capacity,), token_total, jnp.int32).at[targets].set(sources)
    return (targets.reshape(token_total, top_count), owners)

def attention_branch(normalized_rows, segment_ids, query_matrix, key_matrix, value_matrix, w_out):
    token_total = normalized_rows.shape[0]
    query_rows = rounded_pair(matrix_product(normalized_rows, query_matrix)).reshape(token_total, KEY_VALUE_HEADS, QUERY_HEADS // KEY_VALUE_HEADS, HEAD_SIZE)
    key_rows_full = rounded_pair(matrix_product(normalized_rows, key_matrix)).reshape(token_total, KEY_VALUE_HEADS, HEAD_SIZE)
    value_rows_full = rounded_pair(matrix_product(normalized_rows, value_matrix)).reshape(token_total, KEY_VALUE_HEADS, HEAD_SIZE)
    places = jnp.arange(token_total, dtype=jnp.int32)
    allowed = (places[:, None] >= places[None, :]) & (segment_ids[:, None] == segment_ids[None, :])
    scores = low_back(jnp.einsum('qgrd,kgd->grqk', query_rows, key_rows_full, precision=highest) * HEAD_SIZE ** (-0.5))
    scores = jnp.where(allowed[None, None], scores, masked_score)
    shifted = jnp.exp(scores - lax.optimization_barrier(jnp.max(scores, axis=-1, keepdims=True)))
    soft_weights = low(shifted / lax.optimization_barrier(jnp.sum(shifted, axis=-1, keepdims=True)))
    mixed_heads = jnp.einsum('grqk,kgd->qgrd', soft_weights, value_rows_full, precision=highest).reshape(token_total, QUERY_HEADS * HEAD_SIZE)
    return low_back(matrix_product(rounded_pair(mixed_heads), w_out))

def expert_branch(normalized_rows, route_ids, w_router, w_gate, w_up, w_down):
    feature_count = normalized_rows.shape[1]
    gates = route_gates(matrix_product(normalized_rows, w_router), route_ids)
    targets, owners = dispatch_tables(route_ids, EXPERTS, CAP)
    padded = jnp.concatenate([normalized_rows, jnp.zeros((1, feature_count), normalized_rows.dtype)], axis=0)
    buffer_rows = padded[owners].reshape(EXPERTS, CAP, feature_count)
    gate_pre = low_back(jnp.einsum('ecd,edf->ecf', buffer_rows, w_gate, precision=highest))
    up_pre = low_back(jnp.einsum('ecd,edf->ecf', buffer_rows, w_up, precision=highest))
    hidden_units = low(gate_pre * jax.nn.sigmoid(gate_pre) * up_pre)
    expert_out = low_back(jnp.einsum('ecf,efd->ecd', hidden_units, w_down, precision=highest))
    picked = expert_out.reshape(EXPERTS * CAP, feature_count)[targets]
    return low_back(lax.optimization_barrier(jnp.sum(picked * gates[:, :, None], axis=1)))

def layer_group(rows_in, segment_ids, route_ids, attn_scales, query_matrix, key_matrix, value_matrix, w_out, moe_scales, w_router, w_gate, w_up, w_down):
    normed_one = low(rms_scale(rows_in, attn_scales))
    middle = rows_in + attention_branch(normed_one, segment_ids, query_matrix, key_matrix, value_matrix, w_out)
    normed_two = low(rms_scale(middle, moe_scales))
    return middle + expert_branch(normed_two, route_ids, w_router, w_gate, w_up, w_down)

def reference(tokens, cotangent, segments, routes, attn_gain, query_matrix, key_matrix, value_matrix, w_out, moe_gain, w_router, w_gate, w_up, w_down):
    params = tuple((weight.astype(jnp.float32) for weight in (attn_gain, query_matrix, key_matrix, value_matrix, w_out, moe_gain, w_router, w_gate, w_up, w_down)))
    inputs = tokens.astype(jnp.float32).reshape(N_DP, TOK_DEV, MODEL_WIDTH)
    segment_blocks = segments.reshape(N_DP, TOK_DEV)
    route_blocks = routes.reshape(N_DP, TOK_DEV, K)

    def forward(rows_all, *weights):

        def one_group(pieces):
            return layer_group(pieces[0], pieces[1], pieces[2], *weights)
        return lax.map(jax.checkpoint(one_group), (rows_all, segment_blocks, route_blocks))
    result, pullback = jax.vjp(forward, inputs, *params)
    grads = pullback(cotangent.astype(jnp.float32).reshape(N_DP, TOK_DEV, MODEL_WIDTH))
    return (result.reshape(TOKENS, MODEL_WIDTH).astype(jnp.bfloat16), grads[0].reshape(TOKENS, MODEL_WIDTH), grads[1], grads[2], grads[3], grads[4], grads[5], grads[6], grads[7], grads[8], grads[9], grads[10])
```

```python
import jax
import jax.numpy as jnp
from jax import lax
from jax.sharding import PartitionSpec as P

HEAD_SIZE = 64


norm_eps = 1e-06
masked_score = -1e30


def rms_scale(values, scales):
    return values * lax.rsqrt(jnp.mean(values * values, axis=-1, keepdims=True) + norm_eps) * scales


def dense_gates(logits, mask):
    peak = jnp.max(jnp.where(mask, logits, masked_score), axis=1, keepdims=True)
    shifted = jnp.where(mask, jnp.exp(jnp.minimum(logits - peak, 0.0)), 0.0)
    return shifted / jnp.sum(shifted, axis=1, keepdims=True)


def experts_by_row(weights):
    experts, rows, units = weights.shape
    return jnp.transpose(weights, (1, 0, 2)).reshape(rows, experts * units)


def rows_by_expert(values, experts):
    rows, width = values.shape
    return jnp.transpose(values.reshape(rows, experts, width // experts), (1, 0, 2))


def matmul(left, right):
    return jnp.dot(left, right, preferred_element_type=jnp.float32)


def matmul_nt(left, right):
    return lax.dot_general(left, right, (((1,), (1,)), ((), ())), preferred_element_type=jnp.float32)


def matmul_tn(left, right):
    return lax.dot_general(left, right, (((0,), (0,)), ((), ())), preferred_element_type=jnp.float32)


def gather(values, axis_name):
    return lax.all_gather(values, axis_name, axis=0, tiled=True)


def scatter_sum(values, axis_name):
    return lax.psum_scatter(values, axis_name, scatter_dimension=0, tiled=True)


def per_device(
    tokens,
    cotangent,
    segments,
    routes,
    attn_gain,
    query_matrix,
    key_matrix,
    value_matrix,
    w_out,
    moe_gain,
    w_router,
    w_gate,
    w_up,
    w_down,
):
    bf16 = jnp.bfloat16
    f32 = jnp.float32
    scale = HEAD_SIZE ** (-0.5)
    query_width = query_matrix.shape[1]
    key_width = key_matrix.shape[1]
    joint_width = query_width + 2 * key_width
    out_width = w_out.shape[0]
    experts = w_router.shape[1]
    units = w_gate.shape[2]
    local_width = experts * units
    small_width = experts + 2
    small_pad = -(joint_width + out_width + small_width) % 128
    kv_heads = key_width // HEAD_SIZE
    repeat_count = query_width // key_width
    own_rows = tokens.shape[0]

    small_pack = jnp.concatenate(
        [
            query_matrix,
            key_matrix,
            value_matrix,
            w_out.T,
            w_router,
            attn_gain[:, None],
            moe_gain[:, None],
            jnp.zeros((query_matrix.shape[0], small_pad), bf16),
        ],
        axis=1,
    )
    small_all = gather(small_pack, "dp")
    rows_pack = gather(jnp.concatenate([tokens, cotangent], axis=1), "tensor")
    feature_count = tokens.shape[1]
    x_all = rows_pack[:, :feature_count]
    grad_all = rows_pack[:, feature_count:]

    moe_pack = jnp.concatenate(
        [
            experts_by_row(w_gate),
            experts_by_row(w_up),
            jnp.transpose(w_down, (2, 0, 1)).reshape(w_down.shape[2], local_width),
        ],
        axis=1,
    )
    moe_pack, small_all, rows_pack = lax.optimization_barrier((moe_pack, small_all, rows_pack))
    moe_w = gather(moe_pack, "dp")

    joint_w = small_all[:, :joint_width]
    out_t = small_all[:, joint_width : joint_width + out_width]
    rest = joint_width + out_width
    router_w = small_all[:, rest : rest + experts]
    gain_one = small_all[:, rest + experts].astype(f32)
    gain_two = small_all[:, rest + experts + 1].astype(f32)

    x_rows = tokens.astype(f32)
    normed_all = rms_scale(x_all.astype(f32), gain_one).astype(bf16)
    group_rows = normed_all.shape[0]
    projected = matmul(normed_all, joint_w).astype(bf16)
    query_rows = projected[:, :query_width].reshape(group_rows, kv_heads, repeat_count, HEAD_SIZE)
    key_rows = projected[:, query_width : query_width + key_width].reshape(
        group_rows, kv_heads, HEAD_SIZE
    )
    value_rows = projected[:, query_width + key_width :].reshape(group_rows, kv_heads, HEAD_SIZE)
    places = jnp.arange(group_rows, dtype=jnp.int32)
    allowed = (places[:, None] >= places[None, :]) & (segments[:, None] == segments[None, :])
    scores = (
        jnp.einsum("qgrd,kgd->grqk", query_rows, key_rows, preferred_element_type=f32) * scale
    )
    scores = jnp.where(allowed[None, None], scores, masked_score)
    shifted = jnp.exp(scores - jnp.max(scores, axis=-1, keepdims=True))
    soft_weights = shifted / jnp.sum(shifted, axis=-1, keepdims=True)
    low_weights = soft_weights.astype(bf16)
    attended = (
        jnp.einsum("grqk,kgd->qgrd", low_weights, value_rows, preferred_element_type=f32)
        .reshape(group_rows, query_width)
        .astype(bf16)
    )
    attn_branch = scatter_sum(matmul_nt(attended, out_t), "tensor")
    x_mid = x_rows + attn_branch

    normed_two = rms_scale(x_mid, gain_two).astype(bf16)
    moe_all = gather(normed_two, "tensor")
    logits = matmul(moe_all, router_w)
    numbers = jnp.arange(experts, dtype=jnp.int32)
    mask = jnp.any(routes[:, :, None] == numbers[None, None, :], axis=1)
    gates = dense_gates(logits, mask)
    gates_wide = jnp.repeat(gates, units, axis=1)

    both_pre = matmul(moe_all, moe_w[:, : 2 * local_width])
    down_t = moe_w[:, 2 * local_width :]
    hidden_raw = matmul(grad_all, down_t)
    gate_pre = both_pre[:, :local_width]
    up_pre = both_pre[:, local_width:]
    sig = jax.nn.sigmoid(gate_pre)
    silu = gate_pre * sig
    hidden = silu * up_pre
    gated_hidden = (hidden * gates_wide).astype(bf16)
    hidden_grads = hidden_raw * gates_wide
    gate_pre_grads = (hidden_grads * up_pre * (sig * (1.0 + gate_pre * (1.0 - sig)))).astype(bf16)
    up_pre_grads = (hidden_grads * silu).astype(bf16)
    gate_grads = jnp.sum((hidden * hidden_raw).reshape(group_rows, experts, units), axis=2)
    weighted = gates * gate_grads
    logit_grads = weighted - gates * jnp.sum(weighted, axis=1, keepdims=True)
    pre_grads = jnp.concatenate([gate_pre_grads, up_pre_grads], axis=1)
    moe_input_grads = matmul_nt(pre_grads, moe_w[:, : 2 * local_width]) + matmul_nt(
        logit_grads.astype(bf16), router_w
    )
    moe_row_grads = scatter_sum(moe_input_grads, "tensor")
    moe_branch = scatter_sum(matmul_nt(gated_hidden, down_t).astype(bf16), "tensor").astype(f32)
    result = x_mid + moe_branch

    grad_out = cotangent.astype(f32)
    norm_two_values, norm_two_back = jax.vjp(rms_scale, x_mid, gain_two)
    mid_norm_grads, gain_two_grads = norm_two_back(moe_row_grads)
    mid_grads = grad_out + mid_norm_grads
    branch_all = gather(mid_grads.astype(bf16), "tensor")

    moe_grads = jnp.concatenate(
        [
            matmul_tn(moe_all, pre_grads).astype(bf16),
            matmul_tn(grad_all, gated_hidden).astype(bf16),
        ],
        axis=1,
    )
    moe_grads, branch_all = lax.optimization_barrier((moe_grads, branch_all))
    moe_summed = scatter_sum(moe_grads, "dp").astype(f32)
    router_grads = matmul_tn(moe_all, logit_grads.astype(bf16))

    out_t_grads = matmul_tn(branch_all, attended)
    attended_grads = matmul(branch_all, out_t).astype(bf16)
    out_rows = attended_grads.reshape(group_rows, kv_heads, repeat_count, HEAD_SIZE)
    weight_grads = jnp.einsum(
        "qgrd,kgd->grqk", out_rows, value_rows, preferred_element_type=f32
    )
    inner_sum = jnp.sum(soft_weights * weight_grads, axis=-1, keepdims=True)
    score_grads = (soft_weights * (weight_grads - inner_sum)).astype(bf16)
    query_grads = (
        jnp.einsum("grqk,kgd->qgrd", score_grads, key_rows, preferred_element_type=f32) * scale
    )
    key_grads = (
        jnp.einsum("grqk,qgrd->kgd", score_grads, query_rows, preferred_element_type=f32) * scale
    )
    value_grads = jnp.einsum("grqk,qgrd->kgd", low_weights, out_rows, preferred_element_type=f32)
    projected_grads = jnp.concatenate(
        [
            query_grads.reshape(group_rows, query_width),
            key_grads.reshape(group_rows, key_width),
            value_grads.reshape(group_rows, key_width),
        ],
        axis=1,
    ).astype(bf16)
    normed_grads = matmul_nt(projected_grads, joint_w)
    row_grads_one = scatter_sum(normed_grads.astype(bf16), "tensor").astype(f32)
    norm_one_values, norm_one_back = jax.vjp(rms_scale, x_rows, gain_one)
    x_norm_grads, gain_one_grads = norm_one_back(row_grads_one)
    input_grads = mid_grads + x_norm_grads

    small_grads = jnp.concatenate(
        [
            matmul_tn(normed_all, projected_grads),
            out_t_grads,
            router_grads,
            gain_one_grads[:, None],
            gain_two_grads[:, None],
            jnp.zeros((feature_count, small_pad), f32),
        ],
        axis=1,
    ).astype(bf16)
    small_summed = scatter_sum(small_grads, "dp").astype(f32)
    shared = lax.psum(small_summed[:, rest : rest + small_width], "tensor")
    down_summed = moe_summed[:, 2 * local_width :].reshape(-1, experts, units)
    return (
        result.astype(bf16),
        input_grads,
        shared[:, experts],
        small_summed[:, :query_width],
        small_summed[:, query_width : query_width + key_width],
        small_summed[:, query_width + key_width : joint_width],
        small_summed[:, joint_width:rest].T,
        shared[:, experts + 1],
        shared[:, :experts],
        rows_by_expert(moe_summed[:, :local_width], experts),
        rows_by_expert(moe_summed[:, local_width : 2 * local_width], experts),
        jnp.transpose(down_summed, (1, 2, 0)),
    )


def solution(mesh):
    in_specs = (
        P(("dp", "tensor"), None),
        P(("dp", "tensor"), None),
        P("dp"),
        P("dp", None),
        P("dp"),
        P("dp", "tensor"),
        P("dp", "tensor"),
        P("dp", "tensor"),
        P("tensor", "dp"),
        P("dp"),
        P("dp", None),
        P(None, "dp", "tensor"),
        P(None, "dp", "tensor"),
        P(None, "tensor", "dp"),
    )
    out_specs = (
        P(("dp", "tensor"), None),
        P(("dp", "tensor"), None),
        P("dp"),
        P("dp", "tensor"),
        P("dp", "tensor"),
        P("dp", "tensor"),
        P("tensor", "dp"),
        P("dp"),
        P("dp", None),
        P(None, "dp", "tensor"),
        P(None, "dp", "tensor"),
        P(None, "tensor", "dp"),
    )
    return jax.shard_map(
        per_device, mesh=mesh, in_specs=in_specs, out_specs=out_specs, check_vma=False
    )
```

```python
import functools

import jax
import jax.numpy as jnp
from jax import lax
from jax.experimental import pallas as pl
from jax.experimental.pallas import tpu as pltpu
from jax.sharding import PartitionSpec as P

HEAD_SIZE = 64


norm_eps = 1e-06
masked_score = -1e30


def rms_scale(values, scales):
    return values * lax.rsqrt(jnp.mean(values * values, axis=-1, keepdims=True) + norm_eps) * scales


def dense_gates(logits, mask):
    peak = jnp.max(jnp.where(mask, logits, masked_score), axis=1, keepdims=True)
    shifted = jnp.where(mask, jnp.exp(jnp.minimum(logits - peak, 0.0)), 0.0)
    return shifted / jnp.sum(shifted, axis=1, keepdims=True)


def experts_by_row(weights):
    experts, rows, units = weights.shape
    return jnp.transpose(weights, (1, 0, 2)).reshape(rows, experts * units)


def rows_by_expert(values, experts):
    rows, width = values.shape
    return jnp.transpose(values.reshape(rows, experts, width // experts), (1, 0, 2))


def matmul(left, right):
    return jnp.dot(left, right, preferred_element_type=jnp.float32)


def matmul_nt(left, right):
    return lax.dot_general(left, right, (((1,), (1,)), ((), ())), preferred_element_type=jnp.float32)


def matmul_tn(left, right):
    return lax.dot_general(left, right, (((0,), (0,)), ((), ())), preferred_element_type=jnp.float32)


def gather(values, axis_name):
    return lax.all_gather(values, axis_name, axis=0, tiled=True)


def scatter_sum(values, axis_name):
    return lax.psum_scatter(values, axis_name, scatter_dimension=0, tiled=True)


MESH = pl.DeviceIdType.MESH


def ring_index(place, count):
    half = count // 2
    upper = place // half
    return (1 - upper) * (2 * place) + upper * (2 * (count - 1 - place) + 1)


def ring_place(index, count):
    side = index % 2
    row = index // 2
    return (1 - side) * row + side * (count - 1 - row)


def ring_chunks(widths, pieces):
    total = sum(widths) // 128
    cuts = [total * i // (2 * pieces) * 128 for i in range(2 * pieces + 1)]
    ways = {0: [], 1: []}
    base = 0
    for number, width in enumerate(widths):
        for i in range(2 * pieces):
            low, high = max(cuts[i], base), min(cuts[i + 1], base + width)
            if low < high:
                ways[i // pieces].append((number, low - base, high - low, i // pieces))
        base += width
    ordered = []
    for i in range(max(len(ways[0]), len(ways[1]))):
        ordered += ways[0][i : i + 1] + ways[1][i : i + 1]
    return ordered


def ring_setup(count):
    place = ring_place(lax.axis_index("dp"), count)
    right = ring_index((place + 1) % count, count)
    left = ring_index((place + count - 1) % count, count)
    barrier = pltpu.get_barrier_semaphore()
    for neighbour in (left, right):
        pl.semaphore_signal(barrier, inc=1, device_id={"dp": neighbour}, device_id_type=MESH)
    pl.semaphore_wait(barrier, 2)
    return place, (right, left)


def gather_kernel(count, rows, chunks, arrays, *refs):
    ins, outs = refs[:arrays], refs[arrays : 2 * arrays]
    own_sem, send_sem, recv_sem = refs[2 * arrays :]
    place, targets = ring_setup(count)

    def slot(number, first, width, owner):
        start = pl.multiple_of(ring_index(owner, count) * rows, rows)
        return outs[number].at[pl.ds(start, rows), pl.ds(first, width)]

    own = []
    for number in range(arrays):
        start = pl.multiple_of(lax.axis_index("dp") * rows, rows)
        copy = pltpu.make_async_copy(
            ins[number], outs[number].at[pl.ds(start, rows), :], own_sem.at[number]
        )
        copy.start()
        own.append(copy)
    sent = {}
    for step in range(count - 1):
        for c, (number, first, width, way) in enumerate(chunks):
            owner = (place + (step if way else count - step)) % count
            if step == 0:
                source = ins[number].at[:, pl.ds(first, width)]
            else:
                sent[c, step - 1].wait_recv()
                source = slot(number, first, width, owner)
            if step >= 2:
                sent[c, step - 2].wait_send()
            copy = pltpu.make_async_remote_copy(
                src_ref=source,
                dst_ref=slot(number, first, width, owner),
                send_sem=send_sem.at[c, step % 2],
                recv_sem=recv_sem.at[c, step],
                device_id={"dp": targets[way]},
                device_id_type=MESH,
            )
            copy.start()
            sent[c, step] = copy
    for c in range(len(chunks)):
        sent[c, count - 2].wait_recv()
        for step in range(max(0, count - 3), count - 1):
            sent[c, step].wait_send()
    for copy in own:
        copy.wait()


def ring_gather(arrays, count):
    rows = arrays[0].shape[0]
    chunks = ring_chunks([a.shape[1] for a in arrays], 2)
    return pl.pallas_call(
        functools.partial(gather_kernel, count, rows, chunks, len(arrays)),
        out_shape=[jax.ShapeDtypeStruct((count * rows, a.shape[1]), a.dtype) for a in arrays],
        in_specs=[pl.BlockSpec(memory_space=pl.ANY)] * len(arrays),
        out_specs=[pl.BlockSpec(memory_space=pl.ANY)] * len(arrays),
        scratch_shapes=[
            pltpu.SemaphoreType.DMA((len(arrays),)),
            pltpu.SemaphoreType.DMA((len(chunks), 2)),
            pltpu.SemaphoreType.DMA((len(chunks), count - 1)),
        ],
        compiler_params=pltpu.CompilerParams(collective_id=0, has_side_effects=True),
    )(*arrays)


def reduce_kernel(count, rows, chunks, arrays, *refs):
    ins, outs = refs[:arrays], refs[arrays : 2 * arrays]
    held = refs[2 * arrays : 2 * arrays + len(chunks)]
    send_sem, recv_sem = refs[2 * arrays + len(chunks) :]
    place, targets = ring_setup(count)
    tile = 16

    def block(number, first, width, owner):
        start = pl.multiple_of(ring_index(owner, count) * rows, rows)
        return ins[number].at[pl.ds(start, rows), pl.ds(first, width)]

    def add_block(target, arrived, own):
        @pl.loop(0, rows // tile)
        def _(i):
            part = pl.ds(pl.multiple_of(i * tile, tile), tile)
            total = arrived[part, :].astype(jnp.float32) + own[part, :].astype(jnp.float32)
            target[part, :] = total.astype(target.dtype)

    sent = {}
    for step in range(count - 1):
        for c, (number, first, width, way) in enumerate(chunks):
            owner = (place + (1 + step if way else 2 * count - 1 - step)) % count
            own = block(number, first, width, owner)
            source = own
            if step > 0:
                sent[c, step - 1].wait_recv()
                source = held[c].at[step - 1]
                add_block(source, source, own)
            if step >= 2:
                sent[c, step - 2].wait_send()
            copy = pltpu.make_async_remote_copy(
                src_ref=source,
                dst_ref=held[c].at[step],
                send_sem=send_sem.at[c, step % 2],
                recv_sem=recv_sem.at[c, step],
                device_id={"dp": targets[way]},
                device_id_type=MESH,
            )
            copy.start()
            sent[c, step] = copy
    for c, (number, first, width, way) in enumerate(chunks):
        sent[c, count - 2].wait_recv()
        add_block(
            outs[number].at[:, pl.ds(first, width)],
            held[c].at[count - 2],
            block(number, first, width, place),
        )
        for step in range(max(0, count - 3), count - 1):
            sent[c, step].wait_send()


def ring_reduce(arrays, count):
    rows = arrays[0].shape[0] // count
    chunks = ring_chunks([a.shape[1] for a in arrays], 2)
    return pl.pallas_call(
        functools.partial(reduce_kernel, count, rows, chunks, len(arrays)),
        out_shape=[jax.ShapeDtypeStruct((rows, a.shape[1]), jnp.float32) for a in arrays],
        in_specs=[pl.BlockSpec(memory_space=pltpu.VMEM)] * len(arrays),
        out_specs=[pl.BlockSpec(memory_space=pltpu.VMEM)] * len(arrays),
        scratch_shapes=[
            pltpu.VMEM((count - 1, rows, width), jnp.bfloat16) for _, _, width, _ in chunks
        ]
        + [
            pltpu.SemaphoreType.DMA((len(chunks), 2)),
            pltpu.SemaphoreType.DMA((len(chunks), count - 1)),
        ],
        compiler_params=pltpu.CompilerParams(
            collective_id=1, has_side_effects=True, vmem_limit_bytes=56 * 1024 * 1024
        ),
    )(*arrays)


def per_device(
    dp_count,
    tokens,
    cotangent,
    segments,
    routes,
    attn_gain,
    query_matrix,
    key_matrix,
    value_matrix,
    w_out,
    moe_gain,
    w_router,
    w_gate,
    w_up,
    w_down,
):
    bf16 = jnp.bfloat16
    f32 = jnp.float32
    scale = HEAD_SIZE ** (-0.5)
    query_width = query_matrix.shape[1]
    key_width = key_matrix.shape[1]
    joint_width = query_width + 2 * key_width
    out_width = w_out.shape[0]
    experts = w_router.shape[1]
    units = w_gate.shape[2]
    local_width = experts * units
    small_width = experts + 2
    small_pad = -(joint_width + out_width + small_width) % 128
    kv_heads = key_width // HEAD_SIZE
    repeat_count = query_width // key_width
    own_rows = tokens.shape[0]

    small_pack = jnp.concatenate(
        [
            query_matrix,
            key_matrix,
            value_matrix,
            w_out.T,
            w_router,
            attn_gain[:, None],
            moe_gain[:, None],
            jnp.zeros((query_matrix.shape[0], small_pad), bf16),
        ],
        axis=1,
    )
    rows_pack = gather(jnp.concatenate([tokens, cotangent], axis=1), "tensor")
    feature_count = tokens.shape[1]
    x_all = rows_pack[:, :feature_count]
    grad_all = rows_pack[:, feature_count:]

    gate_up_pack = jnp.concatenate([experts_by_row(w_gate), experts_by_row(w_up)], axis=1)
    down_pack = jnp.transpose(w_down, (2, 0, 1)).reshape(w_down.shape[2], local_width)
    small_all, gate_up_t, down_t = ring_gather([small_pack, gate_up_pack, down_pack], dp_count)

    joint_w = small_all[:, :joint_width]
    out_t = small_all[:, joint_width : joint_width + out_width]
    rest = joint_width + out_width
    router_w = small_all[:, rest : rest + experts]
    gain_one = small_all[:, rest + experts].astype(f32)
    gain_two = small_all[:, rest + experts + 1].astype(f32)

    x_rows = tokens.astype(f32)
    normed_all = rms_scale(x_all.astype(f32), gain_one).astype(bf16)
    group_rows = normed_all.shape[0]
    projected = matmul(normed_all, joint_w).astype(bf16)
    query_rows = projected[:, :query_width].reshape(group_rows, kv_heads, repeat_count, HEAD_SIZE)
    key_rows = projected[:, query_width : query_width + key_width].reshape(
        group_rows, kv_heads, HEAD_SIZE
    )
    value_rows = projected[:, query_width + key_width :].reshape(group_rows, kv_heads, HEAD_SIZE)
    places = jnp.arange(group_rows, dtype=jnp.int32)
    allowed = (places[:, None] >= places[None, :]) & (segments[:, None] == segments[None, :])
    scores = (
        jnp.einsum("qgrd,kgd->grqk", query_rows, key_rows, preferred_element_type=f32) * scale
    )
    scores = jnp.where(allowed[None, None], scores, masked_score)
    shifted = jnp.exp(scores - jnp.max(scores, axis=-1, keepdims=True))
    soft_weights = shifted / jnp.sum(shifted, axis=-1, keepdims=True)
    low_weights = soft_weights.astype(bf16)
    attended = (
        jnp.einsum("grqk,kgd->qgrd", low_weights, value_rows, preferred_element_type=f32)
        .reshape(group_rows, query_width)
        .astype(bf16)
    )
    attn_branch = scatter_sum(matmul_nt(attended, out_t).astype(bf16), "tensor").astype(f32)
    x_mid = x_rows + attn_branch

    normed_two = rms_scale(x_mid, gain_two).astype(bf16)
    moe_all = gather(normed_two, "tensor")
    logits = matmul(moe_all, router_w)
    numbers = jnp.arange(experts, dtype=jnp.int32)
    mask = jnp.any(routes[:, :, None] == numbers[None, None, :], axis=1)
    gates = dense_gates(logits, mask)
    gates_wide = jnp.repeat(gates, units, axis=1)

    both_pre = matmul(moe_all, gate_up_t)
    hidden_raw = matmul(grad_all, down_t)
    gate_pre = both_pre[:, :local_width]
    up_pre = both_pre[:, local_width:]
    sig = jax.nn.sigmoid(gate_pre)
    silu = gate_pre * sig
    hidden = silu * up_pre
    gated_hidden = (hidden * gates_wide).astype(bf16)
    hidden_grads = hidden_raw * gates_wide
    gate_pre_grads = (hidden_grads * up_pre * (sig * (1.0 + gate_pre * (1.0 - sig)))).astype(bf16)
    up_pre_grads = (hidden_grads * silu).astype(bf16)
    gate_grads = jnp.sum((hidden * hidden_raw).reshape(group_rows, experts, units), axis=2)
    weighted = gates * gate_grads
    logit_grads = weighted - gates * jnp.sum(weighted, axis=1, keepdims=True)
    pre_grads = jnp.concatenate([gate_pre_grads, up_pre_grads], axis=1)
    moe_input_grads = matmul_nt(pre_grads, gate_up_t) + matmul_nt(
        logit_grads.astype(bf16), router_w
    )
    moe_row_grads = scatter_sum(moe_input_grads.astype(bf16), "tensor").astype(f32)
    moe_branch = scatter_sum(matmul_nt(gated_hidden, down_t).astype(bf16), "tensor").astype(f32)
    result = x_mid + moe_branch

    grad_out = cotangent.astype(f32)
    norm_two_values, norm_two_back = jax.vjp(rms_scale, x_mid, gain_two)
    mid_norm_grads, gain_two_grads = norm_two_back(moe_row_grads)
    mid_grads = grad_out + mid_norm_grads
    branch_all = gather(mid_grads.astype(bf16), "tensor")

    gate_up_grads = matmul_tn(moe_all, pre_grads).astype(bf16)
    down_grads = matmul_tn(grad_all, gated_hidden).astype(bf16)
    router_grads = matmul_tn(moe_all, logit_grads.astype(bf16))

    out_t_grads = matmul_tn(branch_all, attended)
    attended_grads = matmul(branch_all, out_t).astype(bf16)
    out_rows = attended_grads.reshape(group_rows, kv_heads, repeat_count, HEAD_SIZE)
    weight_grads = jnp.einsum(
        "qgrd,kgd->grqk", out_rows, value_rows, preferred_element_type=f32
    )
    inner_sum = jnp.sum(soft_weights * weight_grads, axis=-1, keepdims=True)
    score_grads = (soft_weights * (weight_grads - inner_sum)).astype(bf16)
    query_grads = (
        jnp.einsum("grqk,kgd->qgrd", score_grads, key_rows, preferred_element_type=f32) * scale
    )
    key_grads = (
        jnp.einsum("grqk,qgrd->kgd", score_grads, query_rows, preferred_element_type=f32) * scale
    )
    value_grads = jnp.einsum("grqk,qgrd->kgd", low_weights, out_rows, preferred_element_type=f32)
    projected_grads = jnp.concatenate(
        [
            query_grads.reshape(group_rows, query_width),
            key_grads.reshape(group_rows, key_width),
            value_grads.reshape(group_rows, key_width),
        ],
        axis=1,
    ).astype(bf16)
    normed_grads = matmul_nt(projected_grads, joint_w)
    row_grads_one = scatter_sum(normed_grads.astype(bf16), "tensor").astype(f32)
    norm_one_values, norm_one_back = jax.vjp(rms_scale, x_rows, gain_one)
    x_norm_grads, gain_one_grads = norm_one_back(row_grads_one)
    input_grads = mid_grads + x_norm_grads

    small_grads = jnp.concatenate(
        [
            matmul_tn(normed_all, projected_grads),
            out_t_grads,
            router_grads,
            gain_one_grads[:, None],
            gain_two_grads[:, None],
            jnp.zeros((feature_count, small_pad), f32),
        ],
        axis=1,
    ).astype(bf16)
    small_summed, gate_up_summed, down_summed = ring_reduce(
        [small_grads, gate_up_grads, down_grads], dp_count
    )
    shared = lax.psum(small_summed[:, rest : rest + small_width], "tensor")
    down_summed = down_summed.reshape(-1, experts, units)
    return (
        result.astype(bf16),
        input_grads,
        shared[:, experts],
        small_summed[:, :query_width],
        small_summed[:, query_width : query_width + key_width],
        small_summed[:, query_width + key_width : joint_width],
        small_summed[:, joint_width:rest].T,
        shared[:, experts + 1],
        shared[:, :experts],
        rows_by_expert(gate_up_summed[:, :local_width], experts),
        rows_by_expert(gate_up_summed[:, local_width : 2 * local_width], experts),
        jnp.transpose(down_summed, (1, 2, 0)),
    )


def solution(mesh):
    in_specs = (
        P(("dp", "tensor"), None),
        P(("dp", "tensor"), None),
        P("dp"),
        P("dp", None),
        P("dp"),
        P("dp", "tensor"),
        P("dp", "tensor"),
        P("dp", "tensor"),
        P("tensor", "dp"),
        P("dp"),
        P("dp", None),
        P(None, "dp", "tensor"),
        P(None, "dp", "tensor"),
        P(None, "tensor", "dp"),
    )
    out_specs = (
        P(("dp", "tensor"), None),
        P(("dp", "tensor"), None),
        P("dp"),
        P("dp", "tensor"),
        P("dp", "tensor"),
        P("dp", "tensor"),
        P("tensor", "dp"),
        P("dp"),
        P("dp", None),
        P(None, "dp", "tensor"),
        P(None, "dp", "tensor"),
        P(None, "tensor", "dp"),
    )
    return jax.shard_map(
        functools.partial(per_device, mesh.shape["dp"]), mesh=mesh, in_specs=in_specs, out_specs=out_specs, check_vma=False
    )
```
